32 devices in a mesh: basis: 8 (over y, x, core), ex: 4 (over z).
Axes of the slice: x: 2, y: 2, z: 4, core: 2. Of those that a mesh axis runs over, the one named last changes fastest.
Arguments:
- grad_out: bfloat16 [768, 13824], P('ex', 'basis'), may hold values from -6 to 6
- acts: bfloat16 [768, 5120], P('basis', 'ex'), may hold values from -6 to 6
- basis_out: bfloat16 [13824, 13824], P('basis', 'ex'), may hold values from -0.0546875 to 0.0546875
- basis_in: bfloat16 [5120, 5120], P('ex', 'basis'), may hold values from -0.078125 to 0.078125
- eigvals: float32 [13824, 5120], P('ex', 'basis'), may hold values from 0.1 to 10
- counts: int32 [48], replicated, may hold values from 1 to 16, as said below
Outputs:
- scores: float32 [16, 32], replicated
The draws below stay inside these ranges and needn't reach their ends.
Inputs may be any that keep to these rules, and one draw needn't show every extreme that they name: `counts`: every draw holds some example with exactly 16 tokens in use.
All inputs are finite; a program needn't handle non-finite values.
Results may differ from the reference program's by a relative error of at most 0.0055.
Values may be sent and summed in bfloat16 or wider, within the bound.
A program may use at most 128 MiB of HBM per device.

```python
import math
import jax
import jax.numpy as jnp
from jax import lax

D = 5120
FF = 13824
NQ = 16
NT = 32
TOKX = 16
NTOK = 768


def draw_counts(key, part):
    key = jax.random.fold_in(key, 7)
    first, second = jax.random.split(key)
    values = jax.random.randint(first, (NQ + NT,), 1, TOKX + 1)
    picked = jax.random.randint(second, (), 0, NQ + NT)
    return jnp.where(jnp.arange(NQ + NT) == picked, TOKX, values).astype(jnp.int32)


def block_levels(own_key, dims, cuts, least, largest):
    factor_of, own = 1.0, jax.random.fold_in(own_key, 6)
    for position, shards_of in cuts:
        heights = jnp.exp(jax.random.uniform(jax.random.fold_in(own, position), (shards_of,), jnp.float32, least / len(cuts), largest / len(cuts)))
        factor_of = factor_of * jnp.repeat(heights, dims[position] // shards_of).reshape([-1 if axis == position else 1 for axis in range(len(dims))])
    return factor_of


def noise(key, shape, spread, limit, cuts=(), kind=jnp.bfloat16):
    array = spread * jax.random.normal(key, shape, jnp.float32)
    if cuts:
        array = array * block_levels(key, shape, cuts, -0.22, 0.18)
    return jnp.clip(array, -limit, limit).astype(kind)


def setup_inputs(seed: int = 0) -> dict:
    arg_keys = jax.random.split(jax.random.key(seed), 7)
    grad_out = noise(arg_keys[0], (NTOK, FF), 1.0, 6.0, ((0, 4), (1, 8)))
    acts = noise(arg_keys[1], (NTOK, D), 1.0, 6.0, ((0, 8), (1, 4)))
    basis_out = noise(arg_keys[2], (FF, FF), FF ** -0.5, 0.0546875, ((0, 8), (1, 4)))
    basis_in = noise(arg_keys[3], (D, D), D ** -0.5, 0.078125, ((0, 4), (1, 8)))
    eigvals = jnp.clip(jnp.exp(math.log(10.0) - 4.6051702 * jax.random.uniform(arg_keys[4], (FF, D), jnp.float32) ** block_levels(arg_keys[4], (FF, D), ((0, 4), (1, 8)), -0.2, 0.2)), 0.1, 10.0)
    counts = draw_counts(jax.random.fold_in(arg_keys[6], 71), 0)
    return {"grad_out": grad_out, "acts": acts, "basis_out": basis_out, "basis_in": basis_in, "eigvals": eigvals, "counts": counts}


def reference(grad_out, acts, basis_out, basis_in, eigvals, counts):
    slots = jnp.arange(NTOK, dtype=jnp.int32)
    mask = (slots % TOKX < jnp.repeat(counts, TOKX)).astype(jnp.float32)
    rot_grad = (jnp.dot(grad_out, basis_out, preferred_element_type=jnp.float32) * mask[:, None]).astype(jnp.bfloat16)
    rot_act = jnp.dot(acts, basis_in, preferred_element_type=jnp.float32).astype(jnp.bfloat16)
    query_grad = rot_grad[:NQ * TOKX].reshape(NQ, TOKX, FF)
    query_act = rot_act[:NQ * TOKX].reshape(NQ, TOKX, D)
    train_grad = rot_grad[NQ * TOKX:]
    train_act = rot_act[NQ * TOKX:]

    def one_query(pair):
        grad_q, act_q = pair
        outer = jnp.dot(grad_q.T, act_q, preferred_element_type=jnp.float32)
        precond = (outer / eigvals).astype(jnp.bfloat16)
        projected = lax.dot_general(train_act, precond, (((1,), (1,)), ((), ())), preferred_element_type=jnp.float32)
        return lax.optimization_barrier(jnp.sum((projected * train_grad).reshape(NT, TOKX * FF), axis=1))
    raw = lax.map(one_query, (query_grad, query_act))
    return raw / (TOKX * jnp.sqrt(jnp.float32(FF) * jnp.float32(D)))
```

```python
import functools

import jax
import jax.numpy as jnp
from jax import lax
from jax.experimental import pallas as pl
from jax.experimental.pallas import tpu as pltpu
from jax.sharding import PartitionSpec as P

D = 5120
FF = 13824
NQ = 16
NT = 32
TOKX = 16
NTOK = 768
NQROWS = NQ * TOKX
LANE = 128
TILE = 512


def score_tile(o0, size, g_ref, e_ref, out_ref, gqt, ablk, recip, prec, at):
    fi = e_ref.shape[1]
    ntrain = at.shape[0]
    recip[:size, :] = 1.0 / e_ref[pl.ds(o0, size), :]
    gq = g_ref[:NQROWS, pl.ds(o0, size)].astype(jnp.float32)
    gqt[:size, :] = gq.T.astype(jnp.bfloat16)

    def pair(j, carry):
        outer = jnp.dot(gqt[:size, :], ablk[j], preferred_element_type=jnp.float32)
        for h in range(2):
            cols = slice(h * fi, (h + 1) * fi)
            prec[:size, cols] = (outer[:, cols] * recip[:size, :]).astype(jnp.bfloat16)
        proj = jnp.dot(
            g_ref[NQROWS:, pl.ds(o0, size)], prec[:size, :], preferred_element_type=jnp.float32
        )
        for h in range(2):
            prod = proj[:, h * fi : (h + 1) * fi] * at[...]
            part = prod[:, :LANE]
            for k in range(1, fi // LANE):
                part = part + prod[:, k * LANE : (k + 1) * LANE]
            out_ref[2 * j + h] += jnp.sum(part.reshape(ntrain // TOKX, TOKX, LANE), axis=1)
        return carry

    lax.fori_loop(0, NQ // 2, pair, 0)


def score_kernel(g_ref, a_ref, e_ref, out_ref, gqt, ablk, recip, prec, at):
    fo, fi = e_ref.shape
    out_ref[...] = jnp.zeros_like(out_ref)
    qa = a_ref[:NQROWS, :].astype(jnp.float32)
    owner = lax.broadcasted_iota(jnp.int32, (NQROWS, fi), 0) // TOKX

    def mask_pair(j, carry):
        for h in range(2):
            ablk[j, :, h * fi : (h + 1) * fi] = jnp.where(owner == 2 * j + h, qa, 0.0).astype(
                jnp.bfloat16
            )
        return carry

    lax.fori_loop(0, NQ // 2, mask_pair, 0)
    at[...] = a_ref[NQROWS:, :].astype(jnp.float32)
    refs = (g_ref, e_ref, out_ref, gqt, ablk, recip, prec, at)
    whole = fo // TILE

    def step(i, carry):
        score_tile(pl.multiple_of(i * TILE, TILE), TILE, *refs)
        return carry

    lax.fori_loop(0, whole, step, 0)
    if fo % TILE:
        score_tile(whole * TILE, fo % TILE, *refs)


def local_scores(rot_grad, rot_act, eigvals):
    fo, fi = eigvals.shape
    ntrain = rot_grad.shape[0] - NQROWS
    vmem = pl.BlockSpec(memory_space=pltpu.VMEM)
    sums = pl.pallas_call(
        score_kernel,
        out_shape=jax.ShapeDtypeStruct((NQ, NT, LANE), jnp.float32),
        in_specs=[vmem] * 3,
        out_specs=vmem,
        scratch_shapes=[
            pltpu.VMEM((TILE, NQROWS), jnp.bfloat16),
            pltpu.VMEM((NQ // 2, NQROWS, 2 * fi), jnp.bfloat16),
            pltpu.VMEM((TILE, fi), jnp.float32),
            pltpu.VMEM((TILE, 2 * fi), jnp.bfloat16),
            pltpu.VMEM((ntrain, fi), jnp.float32),
        ],
        compiler_params=pltpu.CompilerParams(vmem_limit_bytes=56 * 1024 * 1024),
    )(rot_grad, rot_act, eigvals)
    return jnp.sum(sums, axis=-1)


def plain_scores(rot_grad, rot_act, eigvals):
    cols_grad = rot_grad.shape[1]
    cols_act = rot_act.shape[1]
    query_grad = rot_grad[:NQROWS].reshape(NQ, TOKX, cols_grad)
    query_act = rot_act[:NQROWS].reshape(NQ, TOKX, cols_act)
    train_grad = rot_grad[NQROWS:]
    train_act = rot_act[NQROWS:]

    def one_query(pair):
        grad_q, act_q = pair
        outer = lax.dot_general(
            grad_q, act_q, (((0,), (0,)), ((), ())), preferred_element_type=jnp.float32
        )
        precond = (outer / eigvals).astype(jnp.bfloat16)
        projected = lax.dot_general(
            train_act, precond, (((1,), (1,)), ((), ())), preferred_element_type=jnp.float32
        )
        return jnp.sum((projected * train_grad).reshape(NT, TOKX * cols_grad), axis=1)

    return lax.map(one_query, (query_grad, query_act))


def body(grad_out, acts, basis_out, basis_in, eigvals, counts):
    partial_grad = jnp.dot(
        lax.all_gather(grad_out, "ex", axis=0, tiled=True),
        basis_out,
        preferred_element_type=jnp.float32,
    )
    partial_act = jnp.dot(
        lax.all_gather(acts, "basis", axis=0, tiled=True),
        basis_in,
        preferred_element_type=jnp.float32,
    )
    slots = jnp.arange(NTOK, dtype=jnp.int32)
    mask = (slots % TOKX < jnp.repeat(counts, TOKX)).astype(jnp.float32)
    summed_grad = lax.psum(partial_grad, "basis")
    rot_grad = (summed_grad * mask[:, None]).astype(jnp.bfloat16)
    rot_act = lax.psum(partial_act, "ex").astype(jnp.bfloat16)
    fo, fi = eigvals.shape
    aligned = fo % LANE == 0 and fi % LANE == 0
    raw = (local_scores if aligned else plain_scores)(rot_grad, rot_act, eigvals)
    scaled = raw / (TOKX * jnp.sqrt(jnp.float32(FF) * jnp.float32(D)))
    return lax.psum(scaled, ("basis", "ex"))


def solution(mesh):
    return jax.shard_map(
        body,
        mesh=mesh,
        in_specs=(
            P("ex", "basis"),
            P("basis", "ex"),
            P("basis", "ex"),
            P("ex", "basis"),
            P("ex", "basis"),
            P(),
        ),
        out_specs=P(),
        check_vma=False,
    )
```

```python
import functools

import jax
import jax.numpy as jnp
from jax import lax
from jax.experimental import pallas as pl
from jax.experimental.pallas import tpu as pltpu
from jax.sharding import PartitionSpec as P

D = 5120
FF = 13824
NQ = 16
NT = 32
TOKX = 16
NTOK = 768
NQROWS = NQ * TOKX
LANE = 128
TILE = 512


def score_tile(o0, size, g_ref, e_ref, out_ref, gqt, ablk, recip, prec, at):
    fi = e_ref.shape[1]
    ntrain = at.shape[0]
    recip[:size, :] = 1.0 / e_ref[pl.ds(o0, size), :]
    gq = g_ref[:NQROWS, pl.ds(o0, size)].astype(jnp.float32)
    gqt[:size, :] = gq.T.astype(jnp.bfloat16)

    def pair(j, carry):
        outer = jnp.dot(gqt[:size, :], ablk[j], preferred_element_type=jnp.float32)
        for h in range(2):
            cols = slice(h * fi, (h + 1) * fi)
            prec[:size, cols] = (outer[:, cols] * recip[:size, :]).astype(jnp.bfloat16)
        proj = jnp.dot(
            g_ref[NQROWS:, pl.ds(o0, size)], prec[:size, :], preferred_element_type=jnp.float32
        )
        for h in range(2):
            prod = proj[:, h * fi : (h + 1) * fi] * at[...]
            part = prod[:, :LANE]
            for k in range(1, fi // LANE):
                part = part + prod[:, k * LANE : (k + 1) * LANE]
            out_ref[2 * j + h] += jnp.sum(part.reshape(ntrain // TOKX, TOKX, LANE), axis=1)
        return carry

    lax.fori_loop(0, NQ // 2, pair, 0)


def score_kernel(g_ref, a_ref, e_ref, out_ref, gqt, ablk, recip, prec, at):
    fo, fi = e_ref.shape
    out_ref[...] = jnp.zeros_like(out_ref)
    qa = a_ref[:NQROWS, :].astype(jnp.float32)
    owner = lax.broadcasted_iota(jnp.int32, (NQROWS, fi), 0) // TOKX

    def mask_pair(j, carry):
        for h in range(2):
            ablk[j, :, h * fi : (h + 1) * fi] = jnp.where(owner == 2 * j + h, qa, 0.0).astype(
                jnp.bfloat16
            )
        return carry

    lax.fori_loop(0, NQ // 2, mask_pair, 0)
    at[...] = a_ref[NQROWS:, :].astype(jnp.float32)
    refs = (g_ref, e_ref, out_ref, gqt, ablk, recip, prec, at)
    whole = fo // TILE

    def step(i, carry):
        score_tile(pl.multiple_of(i * TILE, TILE), TILE, *refs)
        return carry

    lax.fori_loop(0, whole, step, 0)
    if fo % TILE:
        score_tile(whole * TILE, fo % TILE, *refs)


def local_scores(rot_grad, rot_act, eigvals):
    fo, fi = eigvals.shape
    ntrain = rot_grad.shape[0] - NQROWS
    vmem = pl.BlockSpec(memory_space=pltpu.VMEM)
    sums = pl.pallas_call(
        score_kernel,
        out_shape=jax.ShapeDtypeStruct((NQ, NT, LANE), jnp.float32),
        in_specs=[vmem] * 3,
        out_specs=vmem,
        scratch_shapes=[
            pltpu.VMEM((TILE, NQROWS), jnp.bfloat16),
            pltpu.VMEM((NQ // 2, NQROWS, 2 * fi), jnp.bfloat16),
            pltpu.VMEM((TILE, fi), jnp.float32),
            pltpu.VMEM((TILE, 2 * fi), jnp.bfloat16),
            pltpu.VMEM((ntrain, fi), jnp.float32),
        ],
        compiler_params=pltpu.CompilerParams(vmem_limit_bytes=56 * 1024 * 1024),
    )(rot_grad, rot_act, eigvals)
    return jnp.sum(sums, axis=-1)


def plain_scores(rot_grad, rot_act, eigvals):
    cols_grad = rot_grad.shape[1]
    cols_act = rot_act.shape[1]
    query_grad = rot_grad[:NQROWS].reshape(NQ, TOKX, cols_grad)
    query_act = rot_act[:NQROWS].reshape(NQ, TOKX, cols_act)
    train_grad = rot_grad[NQROWS:]
    train_act = rot_act[NQROWS:]

    def one_query(pair):
        grad_q, act_q = pair
        outer = lax.dot_general(
            grad_q, act_q, (((0,), (0,)), ((), ())), preferred_element_type=jnp.float32
        )
        precond = (outer / eigvals).astype(jnp.bfloat16)
        projected = lax.dot_general(
            train_act, precond, (((1,), (1,)), ((), ())), preferred_element_type=jnp.float32
        )
        return jnp.sum((projected * train_grad).reshape(NT, TOKX * cols_grad), axis=1)

    return lax.map(one_query, (query_grad, query_act))


MESH = pl.DeviceIdType.MESH
CHIPS = 4
CORES = 2
PLANE = CHIPS * CORES
LINE = 4
COLS = 384


def remote(src, dst, send, recv, **where):
    return pltpu.make_async_remote_copy(
        src_ref=src,
        dst_ref=dst,
        send_sem=send,
        recv_sem=recv,
        device_id=where,
        device_id_type=MESH,
    )


def greet(partners):
    barrier = pltpu.get_barrier_semaphore()
    for where in partners:
        pl.semaphore_signal(barrier, inc=1, device_id=where, device_id_type=MESH)
    pl.semaphore_wait(barrier, len(partners))


def rotate_kernel(
    g_ref, a_ref, bo_ref, bi_ref, mask_ref, grad_ref, act_ref,
    gg, aa, part, sib, rsend, rrecv, apart, arecv,
    zs, zr, xs, xr, fs, fr, ss, sr, rs, rr, gs, gr, hs, hr, us, ur, vs, vr,
):
    rows, depth = g_ref.shape
    fo = bo_ref.shape[1]
    quarter = rows // CHIPS
    b = lax.axis_index("basis")
    z = lax.axis_index("ex")
    chip, core = b // CORES, b % CORES
    twin = chip * CORES + 1 - core

    def chip_at(k):
        return lax.rem(chip + k + CHIPS, CHIPS)

    def mate(k):
        return chip_at(k) * CORES + core

    def line_at(k):
        return lax.rem(z + k + LINE, LINE)

    near = z // 2
    mirrored = z * (1 - near) + (LINE - 1 - z) * near

    def shard_at(place):
        m = (mirrored, 1 - mirrored, 2, 3)[place]
        return m * (1 - near) + (LINE - 1 - m) * near

    greet(
        [{"basis": mate(k)} for k in range(1, CHIPS)]
        + [{"basis": twin}]
        + [{"ex": line_at(k)} for k in range(1, LINE)]
    )

    waits = []

    def begin(copy):
        copy.start()
        waits.append(copy)

    for k in (1, 3, 2):
        begin(remote(g_ref, gg.at[z], zs.at[k], zr.at[z], ex=line_at(k)))
    for k in (1, 2, 3):
        begin(remote(a_ref, aa.at[b], xs.at[k], xr.at[k], basis=mate(k)))
    begin(remote(a_ref, aa.at[b], fs.at[0], fr.at[0], basis=twin))
    aa[b] = a_ref[...]

    def multiply(place, src):
        half, slot = place // 2, place % 2

        def chunk(c, carry):
            cols = pl.ds(pl.multiple_of(c * COLS, COLS), COLS)
            part[half, slot, :, cols] = jnp.dot(
                src[...], bo_ref[:, cols], preferred_element_type=jnp.float32
            )
            return carry

        lax.fori_loop(0, fo // COLS, chunk, 0)

    def arrive(place):
        shard = shard_at(place)
        remote(gg.at[shard], gg.at[shard], zs.at[0], zr.at[shard], ex=line_at(1)).wait_recv()
        multiply(place, gg.at[shard])

    def pair_send(half):
        begin(
            remote(part.at[half, 1 - core], sib.at[half], ss.at[half], sr.at[half], basis=twin)
        )

    def pair_sum(half, t):
        at = pl.ds(pl.multiple_of(t * quarter, 16), quarter)
        return part[half, core, at, :] + sib[half, at, :]

    def scatter(half):
        remote(sib.at[half], sib.at[half], ss.at[half], sr.at[half], basis=twin).wait_recv()
        for k in (1, 2, 3):
            rsend[half, k - 1] = pair_sum(half, chip_at(k)).astype(jnp.bfloat16)
            begin(
                remote(
                    rsend.at[half, k - 1], rrecv.at[half, k - 1],
                    rs.at[half, k - 1], rr.at[half, k - 1], basis=mate(k),
                )
            )

    def block(half, c, t):
        even, odd = shard_at(2 * half), shard_at(2 * half + 1)
        shard = even * (1 - c) + odd * c
        return pl.ds(pl.multiple_of(shard * rows + t * quarter, 16), quarter)

    def finish(half):
        total = pair_sum(half, chip)
        for k in (1, 2, 3):
            dst = rrecv.at[half, k - 1]
            remote(dst, dst, rs.at[half, k - 1], rr.at[half, k - 1], basis=twin).wait_recv()
            total = total + rrecv[half, k - 1].astype(jnp.float32)
        mine = block(half, core, chip)
        grad_ref[mine, :] = (total * mask_ref[mine, :]).astype(jnp.bfloat16)
        own = grad_ref.at[mine, :]
        for k in (1, 2, 3):
            begin(remote(own, own, gs.at[half, k], gr.at[half, k], basis=mate(k)))
        begin(remote(own, own, hs.at[half, 0], hr.at[half, 0], basis=twin))

    def forward(half):
        for k in (1, 2, 3):
            got = grad_ref.at[block(half, core, chip_at(-k)), :]
            remote(got, got, gs.at[half, k], gr.at[half, k], basis=twin).wait_recv()
            begin(remote(got, got, hs.at[half, k], hr.at[half, k], basis=twin))

    def settle(half):
        for k in range(CHIPS):
            got = grad_ref.at[block(half, 1 - core, chip_at(-k)), :]
            remote(got, got, hs.at[half, k], hr.at[half, k], basis=twin).wait_recv()

    multiply(0, g_ref)
    for k in (1, 2, 3):
        got = aa.at[mate(-k)]
        remote(got, got, xs.at[k], xr.at[k], basis=twin).wait_recv()
        begin(remote(got, got, fs.at[k], fr.at[k], basis=twin))
    arrive(1)
    pair_send(0)
    for k in range(CHIPS):
        got = aa.at[chip_at(-k) * CORES + 1 - core]
        remote(got, got, fs.at[k], fr.at[k], basis=twin).wait_recv()
    tokens = aa.shape[1]
    for i in range(PLANE):
        apart[i * tokens : (i + 1) * tokens, :] = jnp.dot(
            aa[i], bi_ref[...], preferred_element_type=jnp.float32
        )

    def line_block(t):
        return pl.ds(pl.multiple_of(t * rows, 16), rows)

    for k in (1, 3, 2):
        begin(
            remote(
                apart.at[line_block(line_at(k)), :], arecv.at[k - 1],
                us.at[k - 1], ur.at[k - 1], ex=line_at(k),
            )
        )
    scatter(0)
    arrive(2)
    finish(0)
    arrive(3)
    pair_send(1)
    total = apart[line_block(z), :]
    for k in (1, 2, 3):
        dst = arecv.at[k - 1]
        remote(dst, dst, us.at[k - 1], ur.at[k - 1], ex=line_at(1)).wait_recv()
        total = total + arecv[k - 1]
    act_ref[line_block(z), :] = total.astype(jnp.bfloat16)
    own = act_ref.at[line_block(z), :]
    scatter(1)
    for k in (1, 3, 2):
        begin(remote(own, own, vs.at[k - 1], vr.at[k - 1], ex=line_at(k)))
    forward(0)
    finish(1)
    settle(0)
    forward(1)
    for k in (1, 2, 3):
        got = act_ref.at[line_block(line_at(-k)), :]
        remote(got, got, vs.at[k - 1], vr.at[k - 1], ex=line_at(1)).wait_recv()
    settle(1)
    for copy in waits:
        copy.wait_send()


def rotate(grad_out, acts, basis_out, basis_in, mask):
    rows, depth = grad_out.shape
    tokens, feats = acts.shape
    fo, fi = basis_out.shape[1], basis_in.shape[1]
    total = rows * LINE
    vmem = pl.BlockSpec(memory_space=pltpu.VMEM)
    dma = pltpu.SemaphoreType.DMA
    f32, b16 = jnp.float32, jnp.bfloat16
    return pl.pallas_call(
        rotate_kernel,
        out_shape=(
            jax.ShapeDtypeStruct((total, fo), b16),
            jax.ShapeDtypeStruct((total, fi), b16),
        ),
        in_specs=[vmem] * 5,
        out_specs=(vmem, vmem),
        scratch_shapes=[
            pltpu.VMEM((LINE, rows, depth), b16),
            pltpu.VMEM((PLANE, tokens, feats), b16),
            pltpu.VMEM((2, 2, rows, fo), f32),
            pltpu.VMEM((2, rows, fo), f32),
            pltpu.VMEM((2, 3, rows // CHIPS, fo), b16),
            pltpu.VMEM((2, 3, rows // CHIPS, fo), b16),
            pltpu.VMEM((total, fi), f32),
            pltpu.VMEM((3, rows, fi), f32),
            dma((4,)), dma((4,)),
            dma((4,)), dma((4,)),
            dma((4,)), dma((4,)),
            dma((2,)), dma((2,)),
            dma((2, 3)), dma((2, 3)),
            dma((2, 4)), dma((2, 4)),
            dma((2, 4)), dma((2, 4)),
            dma((3,)), dma((3,)),
            dma((3,)), dma((3,)),
        ],
        compiler_params=pltpu.CompilerParams(
            collective_id=0, has_side_effects=True, vmem_limit_bytes=62 * 1024 * 1024
        ),
        cost_estimate=pl.CostEstimate(
            flops=2 * total * depth * fo, bytes_accessed=30 * 1024 * 1024, transcendentals=0
        ),
    )(grad_out, acts, basis_out, basis_in, mask)


def sum_kernel(x_ref, out_ref, plane, line, ps, pr, ls, lr):
    b = lax.axis_index("basis")
    z = lax.axis_index("ex")
    greet(
        [{"basis": lax.rem(b + k, PLANE)} for k in range(1, PLANE)]
        + [{"ex": lax.rem(z + k, LINE)} for k in range(1, LINE)]
    )
    copies = []
    plane[b] = x_ref[...]
    for k in range(1, PLANE):
        to = lax.rem(b + k, PLANE)
        copies.append(remote(x_ref, plane.at[b], ps.at[k], pr.at[k], basis=to))
        copies[-1].start()
    for k in range(1, PLANE):
        got = plane.at[lax.rem(b - k + PLANE, PLANE)]
        remote(got, got, ps.at[k], pr.at[k], basis=lax.rem(b + 1, PLANE)).wait_recv()
    total = plane[0]
    for i in range(1, PLANE):
        total = total + plane[i]
    line[z] = total
    own = line.at[z]
    for k in range(1, LINE):
        to = lax.rem(z + k, LINE)
        copies.append(remote(own, own, ls.at[k], lr.at[k], ex=to))
        copies[-1].start()
    for k in range(1, LINE):
        got = line.at[lax.rem(z - k + LINE, LINE)]
        remote(got, got, ls.at[k], lr.at[k], ex=lax.rem(z + 1, LINE)).wait_recv()
    total = line[0]
    for i in range(1, LINE):
        total = total + line[i]
    out_ref[...] = total
    for copy in copies:
        copy.wait_send()


def sum_all(x):
    flat = jnp.pad(x.reshape(-1, LANE), ((0, 8 - x.size // LANE), (0, 0)))
    vmem = pl.BlockSpec(memory_space=pltpu.VMEM)
    dma = pltpu.SemaphoreType.DMA
    total = pl.pallas_call(
        sum_kernel,
        out_shape=jax.ShapeDtypeStruct(flat.shape, flat.dtype),
        in_specs=[vmem],
        out_specs=vmem,
        scratch_shapes=[
            pltpu.VMEM((PLANE,) + flat.shape, flat.dtype),
            pltpu.VMEM((LINE,) + flat.shape, flat.dtype),
            dma((PLANE,)), dma((PLANE,)),
            dma((LINE,)), dma((LINE,)),
        ],
        compiler_params=pltpu.CompilerParams(collective_id=1, has_side_effects=True),
    )(flat)
    return total[: x.size // LANE].reshape(x.shape)


def slot_mask(counts):
    slots = jnp.arange(NTOK, dtype=jnp.int32)
    return (slots % TOKX < jnp.repeat(counts, TOKX)).astype(jnp.float32)[:, None]


def fits(mesh, grad_out, acts, eigvals):
    fo, fi = eigvals.shape
    return (
        mesh["basis"] == PLANE
        and mesh["ex"] == LINE
        and fo % COLS == 0
        and fi % LANE == 0
        and grad_out.shape[0] % (16 * CHIPS) == 0
        and acts.shape[0] % 16 == 0
    )


def body(grad_out, acts, basis_out, basis_in, eigvals, counts, mesh):
    scale = TOKX * jnp.sqrt(jnp.float32(FF) * jnp.float32(D))
    if fits(mesh, grad_out, acts, eigvals):
        rot_grad, rot_act = rotate(grad_out, acts, basis_out, basis_in, slot_mask(counts))
        return sum_all(local_scores(rot_grad, rot_act, eigvals) / scale)
    partial_grad = jnp.dot(
        lax.all_gather(grad_out, "ex", axis=0, tiled=True),
        basis_out,
        preferred_element_type=jnp.float32,
    )
    partial_act = jnp.dot(
        lax.all_gather(acts, "basis", axis=0, tiled=True),
        basis_in,
        preferred_element_type=jnp.float32,
    )
    summed_grad = lax.psum(partial_grad, "basis")
    rot_grad = (summed_grad * slot_mask(counts)).astype(jnp.bfloat16)
    rot_act = lax.psum(partial_act, "ex").astype(jnp.bfloat16)
    raw = plain_scores(rot_grad, rot_act, eigvals)
    return lax.psum(raw / scale, ("basis", "ex"))


def solution(mesh):
    return jax.shard_map(
        functools.partial(body, mesh=dict(mesh.shape)),
        mesh=mesh,
        in_specs=(
            P("ex", "basis"),
            P("basis", "ex"),
            P("basis", "ex"),
            P("ex", "basis"),
            P("ex", "basis"),
            P(),
        ),
        out_specs=P(),
        check_vma=False,
    )
```

```python
import functools

import jax
import jax.numpy as jnp
from jax import lax
from jax.experimental import pallas as pl
from jax.experimental.pallas import tpu as pltpu
from jax.sharding import PartitionSpec as P

D = 5120
FF = 13824
NQ = 16
NT = 32
TOKX = 16
NTOK = 768
NQROWS = NQ * TOKX
LANE = 128
TILE = 512


def score_tile(o0, size, first, g_ref, e_ref, out_ref, gqt, ablk, recip, precs, at):
    fi = e_ref.shape[1]
    recip[:size, :] = 1.0 / e_ref[pl.ds(o0, size), :]
    gq = g_ref[:NQROWS, pl.ds(o0, size)].astype(jnp.float32)
    gqt[:size, :] = gq.T.astype(jnp.bfloat16)

    def make(j, prec):
        outer = jnp.dot(gqt[:size, :], ablk[j], preferred_element_type=jnp.float32)
        for h in range(2):
            cols = slice(h * fi, (h + 1) * fi)
            prec[:size, cols] = (outer[:, cols] * recip[:size, :]).astype(jnp.bfloat16)

    def use(j, prec):
        proj = jnp.dot(
            g_ref[first:, pl.ds(o0, size)], prec[:size, :], preferred_element_type=jnp.float32
        )
        for h in range(2):
            prod = proj[:, h * fi : (h + 1) * fi] * at[...]
            part = prod[:, :LANE]
            for k in range(1, fi // LANE):
                part = part + prod[:, k * LANE : (k + 1) * LANE]
            out_ref[2 * j + h] += part

    even, odd = precs
    last = NQ // 2 - 2
    make(0, even)

    def pairs(i, carry):
        use(2 * i, even)
        make(2 * i + 1, odd)
        use(2 * i + 1, odd)
        make(2 * i + 2, even)
        return carry

    lax.fori_loop(0, last // 2, pairs, 0)
    use(last, even)
    make(last + 1, odd)
    use(last + 1, odd)


def score_kernel(first, g_ref, a_ref, e_ref, owner_ref, out_ref, gqt, ablk, recip, even, odd, at):
    fo, fi = e_ref.shape
    out_ref[...] = jnp.zeros_like(out_ref)
    qa = a_ref[:NQROWS, :].astype(jnp.float32)
    owner = jnp.broadcast_to(owner_ref[...], (NQROWS, fi))

    def mask_pair(j, carry):
        for h in range(2):
            ablk[j, :, h * fi : (h + 1) * fi] = jnp.where(owner == 2 * j + h, qa, 0.0).astype(
                jnp.bfloat16
            )
        return carry

    lax.fori_loop(0, NQ // 2, mask_pair, 0)
    at[...] = a_ref[first:, :].astype(jnp.float32)
    refs = (first, g_ref, e_ref, out_ref, gqt, ablk, recip, (even, odd), at)
    whole = fo // TILE

    def step(i, carry):
        score_tile(pl.multiple_of(i * TILE, TILE), TILE, *refs)
        return carry

    lax.fori_loop(0, whole, step, 0)
    if fo % TILE:
        score_tile(whole * TILE, fo % TILE, *refs)


def local_scores(rot_grad, rot_act, eigvals, owner, first):
    fo, fi = eigvals.shape
    ntrain = rot_grad.shape[0] - first
    vmem = pl.BlockSpec(memory_space=pltpu.VMEM)
    sums = pl.pallas_call(
        functools.partial(score_kernel, first),
        out_shape=jax.ShapeDtypeStruct((NQ, ntrain, LANE), jnp.float32),
        in_specs=[vmem] * 4,
        out_specs=vmem,
        scratch_shapes=[
            pltpu.VMEM((TILE, NQROWS), jnp.bfloat16),
            pltpu.VMEM((NQ // 2, NQROWS, 2 * fi), jnp.bfloat16),
            pltpu.VMEM((TILE, fi), jnp.float32),
            pltpu.VMEM((TILE, 2 * fi), jnp.bfloat16),
            pltpu.VMEM((TILE, 2 * fi), jnp.bfloat16),
            pltpu.VMEM((ntrain, fi), jnp.float32),
        ],
        compiler_params=pltpu.CompilerParams(vmem_limit_bytes=56 * 1024 * 1024),
    )(rot_grad, rot_act, eigvals, owner[:NQROWS, None])
    rows = jnp.sum(sums, axis=-1)
    trains = NQ + jnp.arange(NT, dtype=jnp.int32)
    member = owner[first:, None] == trains[None, :]
    return jnp.sum(jnp.where(member[None], rows[:, :, None], 0.0), axis=1)


def plain_scores(rot_grad, rot_act, eigvals):
    cols_grad = rot_grad.shape[1]
    cols_act = rot_act.shape[1]
    query_grad = rot_grad[:NQROWS].reshape(NQ, TOKX, cols_grad)
    query_act = rot_act[:NQROWS].reshape(NQ, TOKX, cols_act)
    train_grad = rot_grad[NQROWS:]
    train_act = rot_act[NQROWS:]

    def one_query(pair):
        grad_q, act_q = pair
        outer = lax.dot_general(
            grad_q, act_q, (((0,), (0,)), ((), ())), preferred_element_type=jnp.float32
        )
        precond = (outer / eigvals).astype(jnp.bfloat16)
        projected = lax.dot_general(
            train_act, precond, (((1,), (1,)), ((), ())), preferred_element_type=jnp.float32
        )
        return jnp.sum((projected * train_grad).reshape(NT, TOKX * cols_grad), axis=1)

    return lax.map(one_query, (query_grad, query_act))


MESH = pl.DeviceIdType.MESH
CHIPS = 4
CORES = 2
PLANE = CHIPS * CORES
LINE = 4
COLS = 384


def remote(src, dst, send, recv, **where):
    return pltpu.make_async_remote_copy(
        src_ref=src,
        dst_ref=dst,
        send_sem=send,
        recv_sem=recv,
        device_id=where,
        device_id_type=MESH,
    )


def greet(partners):
    barrier = pltpu.get_barrier_semaphore()
    for where in partners:
        pl.semaphore_signal(barrier, inc=1, device_id=where, device_id_type=MESH)
    pl.semaphore_wait(barrier, len(partners))


def rotate_kernel(
    g_ref, a_ref, bo_ref, bi_ref, pick_ref, grad_ref, act_ref,
    gg, aa, part, sib, rsend, rrecv, apart, arecv,
    zs, zr, xs, xr, fs, fr, ss, sr, rs, rr, gs, gr, hs, hr, us, ur, vs, vr,
):
    rows = pick_ref.shape[1]
    fo = bo_ref.shape[1]
    quarter = rows // CHIPS
    b = lax.axis_index("basis")
    z = lax.axis_index("ex")
    chip, core = b // CORES, b % CORES
    twin = chip * CORES + 1 - core

    def chip_at(k):
        return lax.rem(chip + k + CHIPS, CHIPS)

    def mate(k):
        return chip_at(k) * CORES + core

    def line_at(k):
        return lax.rem(z + k + LINE, LINE)

    near = z // 2
    mirrored = z * (1 - near) + (LINE - 1 - z) * near

    def shard_at(place):
        m = (mirrored, 1 - mirrored, 2, 3)[place]
        return m * (1 - near) + (LINE - 1 - m) * near

    greet(
        [{"basis": mate(k)} for k in range(1, CHIPS)]
        + [{"basis": twin}]
        + [{"ex": line_at(k)} for k in range(1, LINE)]
    )

    waits = []

    def begin(copy):
        copy.start()
        waits.append(copy)

    gg[z] = jnp.dot(pick_ref[z], g_ref[...], preferred_element_type=jnp.float32).astype(
        jnp.bfloat16
    )
    for k in (1, 3, 2):
        begin(remote(gg.at[z], gg.at[z], zs.at[k], zr.at[z], ex=line_at(k)))
    for k in (1, 2, 3):
        begin(remote(a_ref, aa.at[b], xs.at[k], xr.at[k], basis=mate(k)))
    begin(remote(a_ref, aa.at[b], fs.at[0], fr.at[0], basis=twin))
    aa[b] = a_ref[...]

    def multiply(place, src):
        half, slot = place // 2, place % 2

        def chunk(c, carry):
            cols = pl.ds(pl.multiple_of(c * COLS, COLS), COLS)
            part[half, slot, :, cols] = jnp.dot(
                src[...], bo_ref[:, cols], preferred_element_type=jnp.float32
            )
            return carry

        lax.fori_loop(0, fo // COLS, chunk, 0)

    def arrive(place):
        shard = shard_at(place)
        remote(gg.at[shard], gg.at[shard], zs.at[0], zr.at[shard], ex=line_at(1)).wait_recv()
        multiply(place, gg.at[shard])

    def pair_send(half):
        begin(
            remote(part.at[half, 1 - core], sib.at[half], ss.at[half], sr.at[half], basis=twin)
        )

    def pair_sum(half, t):
        at = pl.ds(pl.multiple_of(t * quarter, 16), quarter)
        return part[half, core, at, :] + sib[half, at, :]

    def scatter(half):
        remote(sib.at[half], sib.at[half], ss.at[half], sr.at[half], basis=twin).wait_recv()
        for k in (1, 2, 3):
            rsend[half, k - 1] = pair_sum(half, chip_at(k)).astype(jnp.bfloat16)
            begin(
                remote(
                    rsend.at[half, k - 1], rrecv.at[half, k - 1],
                    rs.at[half, k - 1], rr.at[half, k - 1], basis=mate(k),
                )
            )

    def block(half, c, t):
        even, odd = shard_at(2 * half), shard_at(2 * half + 1)
        shard = even * (1 - c) + odd * c
        return pl.ds(pl.multiple_of(shard * rows + t * quarter, 16), quarter)

    def finish(half):
        total = pair_sum(half, chip)
        for k in (1, 2, 3):
            dst = rrecv.at[half, k - 1]
            remote(dst, dst, rs.at[half, k - 1], rr.at[half, k - 1], basis=twin).wait_recv()
            total = total + rrecv[half, k - 1].astype(jnp.float32)
        mine = block(half, core, chip)
        grad_ref[mine, :] = total.astype(jnp.bfloat16)
        own = grad_ref.at[mine, :]
        for k in (1, 2, 3):
            begin(remote(own, own, gs.at[half, k], gr.at[half, k], basis=mate(k)))
        begin(remote(own, own, hs.at[half, 0], hr.at[half, 0], basis=twin))

    def forward(half):
        for k in (1, 2, 3):
            got = grad_ref.at[block(half, core, chip_at(-k)), :]
            remote(got, got, gs.at[half, k], gr.at[half, k], basis=twin).wait_recv()
            begin(remote(got, got, hs.at[half, k], hr.at[half, k], basis=twin))

    def settle(half):
        for k in range(CHIPS):
            got = grad_ref.at[block(half, 1 - core, chip_at(-k)), :]
            remote(got, got, hs.at[half, k], hr.at[half, k], basis=twin).wait_recv()

    multiply(0, gg.at[z])
    for k in (1, 2, 3):
        got = aa.at[mate(-k)]
        remote(got, got, xs.at[k], xr.at[k], basis=twin).wait_recv()
        begin(remote(got, got, fs.at[k], fr.at[k], basis=twin))
    arrive(1)
    pair_send(0)
    for k in range(CHIPS):
        got = aa.at[chip_at(-k) * CORES + 1 - core]
        remote(got, got, fs.at[k], fr.at[k], basis=twin).wait_recv()
    tokens, feats = aa.shape[1:]
    per = PLANE // LINE
    for t in range(LINE):
        here = aa[t * per : (t + 1) * per].reshape(per * tokens, feats)
        picked = jnp.dot(pick_ref[t], here, preferred_element_type=jnp.float32)
        apart[t * rows : (t + 1) * rows, :] = jnp.dot(
            picked.astype(jnp.bfloat16), bi_ref[...], preferred_element_type=jnp.float32
        )

    def line_block(t):
        return pl.ds(pl.multiple_of(t * rows, 16), rows)

    for k in (1, 3, 2):
        begin(
            remote(
                apart.at[line_block(line_at(k)), :], arecv.at[k - 1],
                us.at[k - 1], ur.at[k - 1], ex=line_at(k),
            )
        )
    scatter(0)
    arrive(2)
    finish(0)
    arrive(3)
    pair_send(1)
    total = apart[line_block(z), :]
    for k in (1, 2, 3):
        dst = arecv.at[k - 1]
        remote(dst, dst, us.at[k - 1], ur.at[k - 1], ex=line_at(1)).wait_recv()
        total = total + arecv[k - 1]
    act_ref[line_block(z), :] = total.astype(jnp.bfloat16)
    own = act_ref.at[line_block(z), :]
    scatter(1)
    for k in (1, 3, 2):
        begin(remote(own, own, vs.at[k - 1], vr.at[k - 1], ex=line_at(k)))
    forward(0)
    finish(1)
    settle(0)
    forward(1)
    for k in (1, 2, 3):
        got = act_ref.at[line_block(line_at(-k)), :]
        remote(got, got, vs.at[k - 1], vr.at[k - 1], ex=line_at(1)).wait_recv()
    settle(1)
    for copy in waits:
        copy.wait_send()


def rotate(grad_out, acts, basis_out, basis_in, pick, call_id):
    rows, depth = pick.shape[1], grad_out.shape[1]
    tokens, feats = acts.shape
    fo, fi = basis_out.shape[1], basis_in.shape[1]
    total = rows * LINE
    vmem = pl.BlockSpec(memory_space=pltpu.VMEM)
    dma = pltpu.SemaphoreType.DMA
    f32, b16 = jnp.float32, jnp.bfloat16
    return pl.pallas_call(
        rotate_kernel,
        out_shape=(
            jax.ShapeDtypeStruct((total, fo), b16),
            jax.ShapeDtypeStruct((total, fi), b16),
        ),
        in_specs=[vmem] * 5,
        out_specs=(vmem, vmem),
        scratch_shapes=[
            pltpu.VMEM((LINE, rows, depth), b16),
            pltpu.VMEM((PLANE, tokens, feats), b16),
            pltpu.VMEM((2, 2, rows, fo), f32),
            pltpu.VMEM((2, rows, fo), f32),
            pltpu.VMEM((2, 3, rows // CHIPS, fo), b16),
            pltpu.VMEM((2, 3, rows // CHIPS, fo), b16),
            pltpu.VMEM((total, fi), f32),
            pltpu.VMEM((3, rows, fi), f32),
            dma((4,)), dma((4,)),
            dma((4,)), dma((4,)),
            dma((4,)), dma((4,)),
            dma((2,)), dma((2,)),
            dma((2, 3)), dma((2, 3)),
            dma((2, 4)), dma((2, 4)),
            dma((2, 4)), dma((2, 4)),
            dma((3,)), dma((3,)),
            dma((3,)), dma((3,)),
        ],
        compiler_params=pltpu.CompilerParams(
            collective_id=call_id, has_side_effects=True, vmem_limit_bytes=62 * 1024 * 1024
        ),
        cost_estimate=pl.CostEstimate(
            flops=2 * total * depth * fo, bytes_accessed=30 * 1024 * 1024, transcendentals=0
        ),
    )(grad_out, acts, basis_out, basis_in, pick)


def sum_kernel(x_ref, out_ref, plane, line, ps, pr, ls, lr):
    b = lax.axis_index("basis")
    z = lax.axis_index("ex")
    greet(
        [{"basis": lax.rem(b + k, PLANE)} for k in range(1, PLANE)]
        + [{"ex": lax.rem(z + k, LINE)} for k in range(1, LINE)]
    )
    copies = []
    plane[b] = x_ref[...]
    for k in range(1, PLANE):
        to = lax.rem(b + k, PLANE)
        copies.append(remote(x_ref, plane.at[b], ps.at[k], pr.at[k], basis=to))
        copies[-1].start()
    for k in range(1, PLANE):
        got = plane.at[lax.rem(b - k + PLANE, PLANE)]
        remote(got, got, ps.at[k], pr.at[k], basis=lax.rem(b + 1, PLANE)).wait_recv()
    total = plane[0]
    for i in range(1, PLANE):
        total = total + plane[i]
    line[z] = total
    own = line.at[z]
    for k in range(1, LINE):
        to = lax.rem(z + k, LINE)
        copies.append(remote(own, own, ls.at[k], lr.at[k], ex=to))
        copies[-1].start()
    for k in range(1, LINE):
        got = line.at[lax.rem(z - k + LINE, LINE)]
        remote(got, got, ls.at[k], lr.at[k], ex=lax.rem(z + 1, LINE)).wait_recv()
    total = line[0]
    for i in range(1, LINE):
        total = total + line[i]
    out_ref[...] = total
    for copy in copies:
        copy.wait_send()


def sum_all(x):
    flat = jnp.pad(x.reshape(-1, LANE), ((0, 8 - x.size // LANE), (0, 0)))
    vmem = pl.BlockSpec(memory_space=pltpu.VMEM)
    dma = pltpu.SemaphoreType.DMA
    total = pl.pallas_call(
        sum_kernel,
        out_shape=jax.ShapeDtypeStruct(flat.shape, flat.dtype),
        in_specs=[vmem],
        out_specs=vmem,
        scratch_shapes=[
            pltpu.VMEM((PLANE,) + flat.shape, flat.dtype),
            pltpu.VMEM((LINE,) + flat.shape, flat.dtype),
            dma((PLANE,)), dma((PLANE,)),
            dma((LINE,)), dma((LINE,)),
        ],
        compiler_params=pltpu.CompilerParams(collective_id=1, has_side_effects=True),
    )(flat)
    return total[: x.size // LANE].reshape(x.shape)


def slot_mask(counts):
    slots = jnp.arange(NTOK, dtype=jnp.int32)
    return (slots % TOKX < jnp.repeat(counts, TOKX)).astype(jnp.float32)[:, None]


def fits(mesh, grad_out, acts, eigvals):
    fo, fi = eigvals.shape
    return (
        mesh["basis"] == PLANE
        and mesh["ex"] == LINE
        and fo % COLS == 0
        and fi % LANE == 0
        and grad_out.shape[0] % (16 * CHIPS) == 0
        and acts.shape[0] % 16 == 0
        and grad_out.shape[0] * LINE == NTOK
    )


PACKED = 128


def packed_rows(counts):
    used = counts.reshape(LINE, -1)
    per = used.shape[1]
    e = jnp.arange(per, dtype=jnp.int32)
    start = jnp.sum(jnp.where(e[None, None, :] < e[None, :, None], used[:, None, :], 0), axis=2)
    k = jnp.arange(TOKX, dtype=jnp.int32)
    place = jnp.where(k < used[:, :, None], start[:, :, None] + k, -1).reshape(LINE, 1, -1)
    r = jnp.arange(PACKED, dtype=jnp.int32)
    pick = (place == r[None, :, None]).astype(jnp.bfloat16)
    rr = r[None, :, None]
    inside = (rr >= start[:, None, :]) & (rr < (start + used)[:, None, :])
    names = jnp.arange(LINE, dtype=jnp.int32)[:, None] * per + e + 1
    owner = jnp.sum(jnp.where(inside, names[:, None, :], 0), axis=2) - 1
    return pick, owner.reshape(-1)


def kept_rows(counts):
    slots = NTOK // LINE
    use = slot_mask(counts).reshape(LINE, 1, slots)
    pick = jnp.where(jnp.eye(slots, dtype=jnp.bool_)[None], use, 0.0).astype(jnp.bfloat16)
    return pick, jnp.arange(NTOK, dtype=jnp.int32) // TOKX


def body(grad_out, acts, basis_out, basis_in, eigvals, counts, mesh):
    scale = TOKX * jnp.sqrt(jnp.float32(FF) * jnp.float32(D))
    if fits(mesh, grad_out, acts, eigvals):

        def scores(rows_of, first, call_id):
            pick, owner = rows_of(counts)
            rot_grad, rot_act = rotate(grad_out, acts, basis_out, basis_in, pick, call_id)
            return local_scores(rot_grad, rot_act, eigvals, owner, first)

        short = jnp.max(jnp.sum(counts.reshape(LINE, -1), axis=1)) <= PACKED
        raw = lax.cond(
            short,
            lambda: scores(packed_rows, PACKED, 0),
            lambda: scores(kept_rows, NQROWS, 2),
        )
        return sum_all(raw / scale)
    partial_grad = jnp.dot(
        lax.all_gather(grad_out, "ex", axis=0, tiled=True),
        basis_out,
        preferred_element_type=jnp.float32,
    )
    partial_act = jnp.dot(
        lax.all_gather(acts, "basis", axis=0, tiled=True),
        basis_in,
        preferred_element_type=jnp.float32,
    )
    summed_grad = lax.psum(partial_grad, "basis")
    rot_grad = (summed_grad * slot_mask(counts)).astype(jnp.bfloat16)
    rot_act = lax.psum(partial_act, "ex").astype(jnp.bfloat16)
    raw = plain_scores(rot_grad, rot_act, eigvals)
    return lax.psum(raw / scale, ("basis", "ex"))


def solution(mesh):
    return jax.shard_map(
        functools.partial(body, mesh=dict(mesh.shape)),
        mesh=mesh,
        in_specs=(
            P("ex", "basis"),
            P("basis", "ex"),
            P("basis", "ex"),
            P("ex", "basis"),
            P("ex", "basis"),
            P(),
        ),
        out_specs=P(),
        check_vma=False,
    )
```

```python
import functools

import jax
import jax.numpy as jnp
from jax import lax
from jax.experimental import pallas as pl
from jax.experimental.pallas import tpu as pltpu
from jax.sharding import PartitionSpec as P

D = 5120
FF = 13824
NQ = 16
NT = 32
TOKX = 16
NTOK = 768
NQROWS = NQ * TOKX
LANE = 128
TILE = 1024


def score_tile(o0, size, first, g_ref, e_ref, out_ref, gqt, ablk, recip, precs, at):
    fi = e_ref.shape[1]
    recip[:size, :] = 1.0 / e_ref[pl.ds(o0, size), :]
    gq = g_ref[:NQROWS, pl.ds(o0, size)].astype(jnp.float32)
    gqt[:size, :] = gq.T.astype(jnp.bfloat16)

    def make(j, prec):
        outer = jnp.dot(gqt[:size, :], ablk[j], preferred_element_type=jnp.float32)
        for h in range(2):
            cols = slice(h * fi, (h + 1) * fi)
            prec[:size, cols] = (outer[:, cols] * recip[:size, :]).astype(jnp.bfloat16)

    def use(j, prec):
        proj = jnp.dot(
            g_ref[first:, pl.ds(o0, size)], prec[:size, :], preferred_element_type=jnp.float32
        )
        for h in range(2):
            prod = proj[:, h * fi : (h + 1) * fi] * at[...]
            part = prod[:, :LANE]
            for k in range(1, fi // LANE):
                part = part + prod[:, k * LANE : (k + 1) * LANE]
            out_ref[2 * j + h] += part

    even, odd = precs
    last = NQ // 2 - 2
    make(0, even)

    def pairs(i, carry):
        use(2 * i, even)
        make(2 * i + 1, odd)
        use(2 * i + 1, odd)
        make(2 * i + 2, even)
        return carry

    lax.fori_loop(0, last // 2, pairs, 0)
    use(last, even)
    make(last + 1, odd)
    use(last + 1, odd)


def score_kernel(first, g_ref, a_ref, e_ref, owner_ref, out_ref, gqt, ablk, recip, even, odd, at):
    fo, fi = e_ref.shape
    out_ref[...] = jnp.zeros_like(out_ref)
    qa = a_ref[:NQROWS, :].astype(jnp.float32)
    owner = jnp.broadcast_to(owner_ref[...], (NQROWS, fi))

    def mask_pair(j, carry):
        for h in range(2):
            ablk[j, :, h * fi : (h + 1) * fi] = jnp.where(owner == 2 * j + h, qa, 0.0).astype(
                jnp.bfloat16
            )
        return carry

    lax.fori_loop(0, NQ // 2, mask_pair, 0)
    at[...] = a_ref[first:, :].astype(jnp.float32)
    refs = (first, g_ref, e_ref, out_ref, gqt, ablk, recip, (even, odd), at)
    whole = fo // TILE

    def step(i, carry):
        score_tile(pl.multiple_of(i * TILE, TILE), TILE, *refs)
        return carry

    lax.fori_loop(0, whole, step, 0)
    if fo % TILE:
        score_tile(whole * TILE, fo % TILE, *refs)


def local_scores(rot_grad, rot_act, eigvals, owner, first):
    fo, fi = eigvals.shape
    ntrain = rot_grad.shape[0] - first
    vmem = pl.BlockSpec(memory_space=pltpu.VMEM)
    sums = pl.pallas_call(
        functools.partial(score_kernel, first),
        out_shape=jax.ShapeDtypeStruct((NQ, ntrain, LANE), jnp.float32),
        in_specs=[vmem] * 4,
        out_specs=vmem,
        scratch_shapes=[
            pltpu.VMEM((TILE, NQROWS), jnp.bfloat16),
            pltpu.VMEM((NQ // 2, NQROWS, 2 * fi), jnp.bfloat16),
            pltpu.VMEM((TILE, fi), jnp.float32),
            pltpu.VMEM((TILE, 2 * fi), jnp.bfloat16),
            pltpu.VMEM((TILE, 2 * fi), jnp.bfloat16),
            pltpu.VMEM((ntrain, fi), jnp.float32),
        ],
        compiler_params=pltpu.CompilerParams(vmem_limit_bytes=56 * 1024 * 1024),
    )(rot_grad, rot_act, eigvals, owner[:NQROWS, None])
    rows = jnp.sum(sums, axis=-1)
    trains = NQ + jnp.arange(NT, dtype=jnp.int32)
    member = owner[first:, None] == trains[None, :]
    return jnp.sum(jnp.where(member[None], rows[:, :, None], 0.0), axis=1)


def plain_scores(rot_grad, rot_act, eigvals):
    cols_grad = rot_grad.shape[1]
    cols_act = rot_act.shape[1]
    query_grad = rot_grad[:NQROWS].reshape(NQ, TOKX, cols_grad)
    query_act = rot_act[:NQROWS].reshape(NQ, TOKX, cols_act)
    train_grad = rot_grad[NQROWS:]
    train_act = rot_act[NQROWS:]

    def one_query(pair):
        grad_q, act_q = pair
        outer = lax.dot_general(
            grad_q, act_q, (((0,), (0,)), ((), ())), preferred_element_type=jnp.float32
        )
        precond = (outer / eigvals).astype(jnp.bfloat16)
        projected = lax.dot_general(
            train_act, precond, (((1,), (1,)), ((), ())), preferred_element_type=jnp.float32
        )
        return jnp.sum((projected * train_grad).reshape(NT, TOKX * cols_grad), axis=1)

    return lax.map(one_query, (query_grad, query_act))


MESH = pl.DeviceIdType.MESH
CHIPS = 4
CORES = 2
PLANE = CHIPS * CORES
LINE = 4
COLS = 384


def remote(src, dst, send, recv, **where):
    return pltpu.make_async_remote_copy(
        src_ref=src,
        dst_ref=dst,
        send_sem=send,
        recv_sem=recv,
        device_id=where,
        device_id_type=MESH,
    )


def greet(partners):
    barrier = pltpu.get_barrier_semaphore()
    for where in partners:
        pl.semaphore_signal(barrier, inc=1, device_id=where, device_id_type=MESH)
    pl.semaphore_wait(barrier, len(partners))


def rotate_kernel(
    g_ref, a_ref, bo_ref, bi_ref, pick_ref, grad_ref, act_ref,
    gg, aa, part, sib, rsend, rrecv, apart, arecv,
    zs, zr, xs, xr, fs, fr, ss, sr, rs, rr, gs, gr, hs, hr, us, ur, vs, vr,
):
    rows = pick_ref.shape[1]
    fo = bo_ref.shape[1]
    quarter = rows // CHIPS
    b = lax.axis_index("basis")
    z = lax.axis_index("ex")
    chip, core = b // CORES, b % CORES
    twin = chip * CORES + 1 - core

    def chip_at(k):
        return lax.rem(chip + k + CHIPS, CHIPS)

    def mate(k):
        return chip_at(k) * CORES + core

    def line_at(k):
        return lax.rem(z + k + LINE, LINE)

    near = z // 2
    mirrored = z * (1 - near) + (LINE - 1 - z) * near

    def shard_at(place):
        m = (mirrored, 1 - mirrored, 2, 3)[place]
        return m * (1 - near) + (LINE - 1 - m) * near

    greet(
        [{"basis": mate(k)} for k in range(1, CHIPS)]
        + [{"basis": twin}]
        + [{"ex": line_at(k)} for k in range(1, LINE)]
    )

    waits = []

    def begin(copy):
        copy.start()
        waits.append(copy)

    gg[z] = jnp.dot(pick_ref[z], g_ref[...], preferred_element_type=jnp.float32).astype(
        jnp.bfloat16
    )
    up = remote(gg.at[z], gg.at[z], zs.at[z], zr.at[z], ex=line_at(1))
    down = remote(gg.at[z], gg.at[z], zs.at[LINE], zr.at[z], ex=line_at(-1))
    passed = [(up, z < LINE - 1), (down, z > 0)]
    for copy, when in passed:
        pl.when(when)(copy.start)
    for k in (1, 2, 3):
        begin(remote(a_ref, aa.at[b], xs.at[k], xr.at[k], basis=mate(k)))
    begin(remote(a_ref, aa.at[b], fs.at[0], fr.at[0], basis=twin))
    aa[b] = a_ref[...]

    def multiply(place, src):
        half, slot = place // 2, place % 2

        def chunk(c, carry):
            cols = pl.ds(pl.multiple_of(c * COLS, COLS), COLS)
            part[half, slot, :, cols] = jnp.dot(
                src[...], bo_ref[:, cols], preferred_element_type=jnp.float32
            )
            return carry

        lax.fori_loop(0, fo // COLS, chunk, 0)

    def take(place):
        shard = shard_at(place)
        slot = gg.at[shard]
        remote(slot, slot, zs.at[shard], zr.at[shard], ex=line_at(1)).wait_recv()
        for step, when in ((1, (shard < z) & (z < LINE - 1)), (-1, (shard > z) & (z > 0))):
            copy = remote(slot, slot, zs.at[shard], zr.at[shard], ex=line_at(step))
            pl.when(when)(copy.start)
            passed.append((copy, when))

    def pair_send(half):
        begin(
            remote(part.at[half, 1 - core], sib.at[half], ss.at[half], sr.at[half], basis=twin)
        )

    def pair_sum(half, t):
        at = pl.ds(pl.multiple_of(t * quarter, 16), quarter)
        return part[half, core, at, :] + sib[half, at, :]

    def scatter(half):
        remote(sib.at[half], sib.at[half], ss.at[half], sr.at[half], basis=twin).wait_recv()
        for k in (1, 2, 3):
            rsend[half, k - 1] = pair_sum(half, chip_at(k)).astype(jnp.bfloat16)
            begin(
                remote(
                    rsend.at[half, k - 1], rrecv.at[half, k - 1],
                    rs.at[half, k - 1], rr.at[half, k - 1], basis=mate(k),
                )
            )

    def block(half, c, t):
        even, odd = shard_at(2 * half), shard_at(2 * half + 1)
        shard = even * (1 - c) + odd * c
        return pl.ds(pl.multiple_of(shard * rows + t * quarter, 16), quarter)

    def finish(half):
        total = pair_sum(half, chip)
        for k in (1, 2, 3):
            dst = rrecv.at[half, k - 1]
            remote(dst, dst, rs.at[half, k - 1], rr.at[half, k - 1], basis=twin).wait_recv()
            total = total + rrecv[half, k - 1].astype(jnp.float32)
        mine = block(half, core, chip)
        grad_ref[mine, :] = total.astype(jnp.bfloat16)
        own = grad_ref.at[mine, :]
        for k in (1, 2, 3):
            begin(remote(own, own, gs.at[half, k], gr.at[half, k], basis=mate(k)))
        begin(remote(own, own, hs.at[half, 0], hr.at[half, 0], basis=twin))

    def forward(half):
        for k in (1, 2, 3):
            got = grad_ref.at[block(half, core, chip_at(-k)), :]
            remote(got, got, gs.at[half, k], gr.at[half, k], basis=twin).wait_recv()
            begin(remote(got, got, hs.at[half, k], hr.at[half, k], basis=twin))

    def settle(half):
        for k in range(CHIPS):
            got = grad_ref.at[block(half, 1 - core, chip_at(-k)), :]
            remote(got, got, hs.at[half, k], hr.at[half, k], basis=twin).wait_recv()

    def line_block(t):
        return pl.ds(pl.multiple_of(t * rows, 16), rows)

    def rotate_acts():
        for k in range(CHIPS):
            got = aa.at[chip_at(-k) * CORES + 1 - core]
            remote(got, got, fs.at[k], fr.at[k], basis=twin).wait_recv()
        tokens, feats = aa.shape[1:]
        per = PLANE // LINE
        for t in range(LINE):
            here = aa[t * per : (t + 1) * per].reshape(per * tokens, feats)
            picked = jnp.dot(pick_ref[t], here, preferred_element_type=jnp.float32)
            apart[t * rows : (t + 1) * rows, :] = jnp.dot(
                picked.astype(jnp.bfloat16), bi_ref[...], preferred_element_type=jnp.float32
            )
        for k in (1, 3, 2):
            begin(
                remote(
                    apart.at[line_block(line_at(k)), :], arecv.at[k - 1],
                    us.at[k - 1], ur.at[k - 1], ex=line_at(k),
                )
            )

    def finish_acts():
        total = apart[line_block(z), :]
        for k in (1, 2, 3):
            dst = arecv.at[k - 1]
            remote(dst, dst, us.at[k - 1], ur.at[k - 1], ex=line_at(1)).wait_recv()
            total = total + arecv[k - 1]
        act_ref[line_block(z), :] = total.astype(jnp.bfloat16)
        own = act_ref.at[line_block(z), :]
        for k in (1, 3, 2):
            begin(remote(own, own, vs.at[k - 1], vr.at[k - 1], ex=line_at(k)))

    multiply(0, gg.at[z])
    take(1)
    multiply(1, gg.at[shard_at(1)])
    pair_send(0)
    for k in (1, 2, 3):
        got = aa.at[mate(-k)]
        remote(got, got, xs.at[k], xr.at[k], basis=twin).wait_recv()
        begin(remote(got, got, fs.at[k], fr.at[k], basis=twin))
    take(2)
    scatter(0)
    multiply(2, gg.at[shard_at(2)])
    rotate_acts()
    take(3)
    finish(0)
    multiply(3, gg.at[shard_at(3)])
    pair_send(1)
    forward(0)
    scatter(1)
    finish(1)
    finish_acts()
    settle(0)
    forward(1)
    for k in (1, 2, 3):
        got = act_ref.at[line_block(line_at(-k)), :]
        remote(got, got, vs.at[k - 1], vr.at[k - 1], ex=line_at(1)).wait_recv()
    settle(1)
    for copy in waits:
        copy.wait_send()
    for copy, when in passed:
        pl.when(when)(copy.wait_send)


def rotate(grad_out, acts, basis_out, basis_in, pick, call_id):
    rows, depth = pick.shape[1], grad_out.shape[1]
    tokens, feats = acts.shape
    fo, fi = basis_out.shape[1], basis_in.shape[1]
    total = rows * LINE
    vmem = pl.BlockSpec(memory_space=pltpu.VMEM)
    dma = pltpu.SemaphoreType.DMA
    f32, b16 = jnp.float32, jnp.bfloat16
    return pl.pallas_call(
        rotate_kernel,
        out_shape=(
            jax.ShapeDtypeStruct((total, fo), b16),
            jax.ShapeDtypeStruct((total, fi), b16),
        ),
        in_specs=[vmem] * 5,
        out_specs=(vmem, vmem),
        scratch_shapes=[
            pltpu.VMEM((LINE, rows, depth), b16),
            pltpu.VMEM((PLANE, tokens, feats), b16),
            pltpu.VMEM((2, 2, rows, fo), f32),
            pltpu.VMEM((2, rows, fo), f32),
            pltpu.VMEM((2, 3, rows // CHIPS, fo), b16),
            pltpu.VMEM((2, 3, rows // CHIPS, fo), b16),
            pltpu.VMEM((total, fi), f32),
            pltpu.VMEM((3, rows, fi), f32),
            dma((LINE + 1,)), dma((LINE,)),
            dma((4,)), dma((4,)),
            dma((4,)), dma((4,)),
            dma((2,)), dma((2,)),
            dma((2, 3)), dma((2, 3)),
            dma((2, 4)), dma((2, 4)),
            dma((2, 4)), dma((2, 4)),
            dma((3,)), dma((3,)),
            dma((3,)), dma((3,)),
        ],
        compiler_params=pltpu.CompilerParams(
            collective_id=call_id, has_side_effects=True, vmem_limit_bytes=62 * 1024 * 1024
        ),
        cost_estimate=pl.CostEstimate(
            flops=2 * total * depth * fo, bytes_accessed=30 * 1024 * 1024, transcendentals=0
        ),
    )(grad_out, acts, basis_out, basis_in, pick)


def sum_kernel(x_ref, out_ref, plane, line, ps, pr, ls, lr):
    b = lax.axis_index("basis")
    z = lax.axis_index("ex")
    greet(
        [{"basis": lax.rem(b + k, PLANE)} for k in range(1, PLANE)]
        + [{"ex": lax.rem(z + k, LINE)} for k in range(1, LINE)]
    )
    copies = []
    plane[b] = x_ref[...]
    for k in range(1, PLANE):
        to = lax.rem(b + k, PLANE)
        copies.append(remote(x_ref, plane.at[b], ps.at[k], pr.at[k], basis=to))
        copies[-1].start()
    for k in range(1, PLANE):
        got = plane.at[lax.rem(b - k + PLANE, PLANE)]
        remote(got, got, ps.at[k], pr.at[k], basis=lax.rem(b + 1, PLANE)).wait_recv()
    total = plane[0]
    for i in range(1, PLANE):
        total = total + plane[i]
    line[z] = total
    own = line.at[z]
    for k in range(1, LINE):
        to = lax.rem(z + k, LINE)
        copies.append(remote(own, own, ls.at[k], lr.at[k], ex=to))
        copies[-1].start()
    for k in range(1, LINE):
        got = line.at[lax.rem(z - k + LINE, LINE)]
        remote(got, got, ls.at[k], lr.at[k], ex=lax.rem(z + 1, LINE)).wait_recv()
    total = line[0]
    for i in range(1, LINE):
        total = total + line[i]
    out_ref[...] = total
    for copy in copies:
        copy.wait_send()


def sum_all(x):
    flat = jnp.pad(x.reshape(-1, LANE), ((0, 8 - x.size // LANE), (0, 0)))
    vmem = pl.BlockSpec(memory_space=pltpu.VMEM)
    dma = pltpu.SemaphoreType.DMA
    total = pl.pallas_call(
        sum_kernel,
        out_shape=jax.ShapeDtypeStruct(flat.shape, flat.dtype),
        in_specs=[vmem],
        out_specs=vmem,
        scratch_shapes=[
            pltpu.VMEM((PLANE,) + flat.shape, flat.dtype),
            pltpu.VMEM((LINE,) + flat.shape, flat.dtype),
            dma((PLANE,)), dma((PLANE,)),
            dma((LINE,)), dma((LINE,)),
        ],
        compiler_params=pltpu.CompilerParams(collective_id=1, has_side_effects=True),
    )(flat)
    return total[: x.size // LANE].reshape(x.shape)


def slot_mask(counts):
    slots = jnp.arange(NTOK, dtype=jnp.int32)
    return (slots % TOKX < jnp.repeat(counts, TOKX)).astype(jnp.float32)[:, None]


def fits(mesh, grad_out, acts, eigvals):
    fo, fi = eigvals.shape
    return (
        mesh["basis"] == PLANE
        and mesh["ex"] == LINE
        and fo % COLS == 0
        and fi % LANE == 0
        and grad_out.shape[0] % (16 * CHIPS) == 0
        and acts.shape[0] % 16 == 0
        and grad_out.shape[0] * LINE == NTOK
    )


PACKED = 128


def packed_rows(counts):
    used = counts.reshape(LINE, -1)
    per = used.shape[1]
    e = jnp.arange(per, dtype=jnp.int32)
    start = jnp.sum(jnp.where(e[None, None, :] < e[None, :, None], used[:, None, :], 0), axis=2)
    k = jnp.arange(TOKX, dtype=jnp.int32)
    place = jnp.where(k < used[:, :, None], start[:, :, None] + k, -1).reshape(LINE, 1, -1)
    r = jnp.arange(PACKED, dtype=jnp.int32)
    pick = (place == r[None, :, None]).astype(jnp.bfloat16)
    rr = r[None, :, None]
    inside = (rr >= start[:, None, :]) & (rr < (start + used)[:, None, :])
    names = jnp.arange(LINE, dtype=jnp.int32)[:, None] * per + e + 1
    owner = jnp.sum(jnp.where(inside, names[:, None, :], 0), axis=2) - 1
    return pick, owner.reshape(-1)


def kept_rows(counts):
    slots = NTOK // LINE
    use = slot_mask(counts).reshape(LINE, 1, slots)
    pick = jnp.where(jnp.eye(slots, dtype=jnp.bool_)[None], use, 0.0).astype(jnp.bfloat16)
    return pick, jnp.arange(NTOK, dtype=jnp.int32) // TOKX


def body(grad_out, acts, basis_out, basis_in, eigvals, counts, mesh):
    scale = TOKX * jnp.sqrt(jnp.float32(FF) * jnp.float32(D))
    if fits(mesh, grad_out, acts, eigvals):

        def scores(rows_of, first, call_id):
            pick, owner = rows_of(counts)
            rot_grad, rot_act = rotate(grad_out, acts, basis_out, basis_in, pick, call_id)
            return local_scores(rot_grad, rot_act, eigvals, owner, first)

        short = jnp.max(jnp.sum(counts.reshape(LINE, -1), axis=1)) <= PACKED
        raw = lax.cond(
            short,
            lambda: scores(packed_rows, PACKED, 0),
            lambda: scores(kept_rows, NQROWS, 2),
        )
        return sum_all(raw / scale)
    partial_grad = jnp.dot(
        lax.all_gather(grad_out, "ex", axis=0, tiled=True),
        basis_out,
        preferred_element_type=jnp.float32,
    )
    partial_act = jnp.dot(
        lax.all_gather(acts, "basis", axis=0, tiled=True),
        basis_in,
        preferred_element_type=jnp.float32,
    )
    summed_grad = lax.psum(partial_grad, "basis")
    rot_grad = (summed_grad * slot_mask(counts)).astype(jnp.bfloat16)
    rot_act = lax.psum(partial_act, "ex").astype(jnp.bfloat16)
    raw = plain_scores(rot_grad, rot_act, eigvals)
    return lax.psum(raw / scale, ("basis", "ex"))


def solution(mesh):
    return jax.shard_map(
        functools.partial(body, mesh=dict(mesh.shape)),
        mesh=mesh,
        in_specs=(
            P("ex", "basis"),
            P("basis", "ex"),
            P("basis", "ex"),
            P("ex", "basis"),
            P("ex", "basis"),
            P(),
        ),
        out_specs=P(),
        check_vma=False,
    )
```
